32 devices in a mesh: ep: 16 (over z, y, x), dp: 2 (over core).
Axes of the slice: x: 2, y: 2, z: 4, core: 2. Of those that a mesh axis runs over, the one named last changes fastest.
Arguments:
- tokens: bfloat16 [4096, 3584], P(('dp', 'ep')), parts along dimension 0, may hold values from -6 to 6
- routes: int32 [4096, 1], P(('dp', 'ep')), parts along dimension 0, may hold values from 0 to 1; in each aligned block of 128 rows (0 to 127, 128 to 255, ...) at most 72 rows name the same one
- route_weight: float32 [4096, 1], P(('dp', 'ep')), parts along dimension 0, may hold values from 0.1 to 1
- norm_gain: bfloat16 [3584], replicated, may hold values from 0.25 to 1.75
- w_gate: bfloat16 [16, 3584, 128], P('ep'), may hold values from -0.09375 to 0.09375
- w_up: bfloat16 [16, 3584, 128], P('ep'), may hold values from -0.09375 to 0.09375
- w_down: bfloat16 [16, 128, 3584], P('ep'), may hold values from -0.1875 to 0.1875
Outputs:
- mixed: bfloat16 [4096, 3584], P(('dp', 'ep')), parts along dimension 0
The draws below stay inside these ranges and needn't reach their ends.
There are 2 independent parts, one for each index of `dp`. The reference program is written for one: setup_inputs(seed, part) draws one part's arguments, and reference() takes and returns one part's arrays. A program takes and returns all parts, laid end to end along the dimension named above; an argument that names none is the same for every part. Nothing has to cross between parts.
Inputs may be any that keep to these rules, and one draw needn't show every extreme that they name: `routes`: each row names 1 different experts; among the rows of one device at most 72 name any one expert, and in every draw some expert is named by exactly 72 rows of some device.
All inputs are finite; a program needn't handle non-finite values.
Results may differ from the reference program's by a relative error of at most 0.0071.
Values may be sent and summed in bfloat16 or wider, within the bound.
A program may use at most 64 MiB of HBM per device.

```python
import math
import jax
import jax.numpy as jnp
import numpy as np
from jax import lax

D = 3584
FFE = 1024
FFE_DEV = 128
SHARE = 8
EXPERTS = 2
TOPK = 1
TOK_DEV = 128
CAP = 72
TOKENS = 2048
N_EP = 16


def block_levels(key, dims, shards, low, top_value):
    loudness, own = 1.0, jax.random.fold_in(key, 6)
    for dim, parts in shards:
        draws = jnp.exp(jax.random.uniform(jax.random.fold_in(own, dim), (parts,), jnp.float32, low / len(shards), top_value / len(shards)))
        loudness = loudness * jnp.repeat(draws, dims[dim] // parts).reshape([-1 if axis == dim else 1 for axis in range(len(dims))])
    return loudness


def deal_out(rng, own, number, rows, count, top, bound, skew):
    order = jax.random.permutation(rng, count)
    packed, usual = shares(count, rows * top, bound, skew, True), shares(count, rows * top, bound, skew, False)
    places = jnp.arange(count)

    def named(sizes, turn):
        used = int((sizes > 0).sum())
        fixed = max(1, used // 4)
        passed = fixed + (places - fixed + turn * (used - fixed)) % max(1, count - fixed)
        return jnp.zeros((count,), jnp.int32).at[order[jnp.where(places < fixed, places, passed)]].set(jnp.asarray(sizes, jnp.int32))

    sizes = jnp.where(number % 4 == 0, named(packed, number // 4), named(usual, number - number // 4 - 1))
    mixed = jax.random.permutation(jax.random.fold_in(own, 3), count)
    donor, taker = mixed[0:count // 2 * 2:2], mixed[1:count // 2 * 2:2]
    room = jnp.minimum(sizes[donor] - 1, bound - sizes[taker]) // 2
    room = jnp.where((donor == order[0]) | (taker == order[0]) | (sizes[taker] == 0), 0, jnp.maximum(room, 0))
    passed = jax.random.randint(jax.random.fold_in(own, 4), (count // 2,), 0, 1 << 20) % (room + 1)
    sizes = sizes.at[donor].add(-passed).at[taker].add(passed)
    members = jnp.searchsorted(jnp.cumsum(sizes), jnp.arange(rows * top), side="right").astype(jnp.int32)
    table = members.reshape(top, rows).T
    table = table[jax.random.permutation(jax.random.fold_in(own, 1), rows)]
    turn = jax.random.randint(jax.random.fold_in(own, 2), (rows, 1), 0, top)
    return jnp.take_along_axis(table, (jnp.arange(top)[None, :] + turn) % top, axis=1)


def shares(amount, total, most, lean, full):
    portions = [(1 << 20) // math.isqrt(grade ** lean) + 1 for grade in range(1, amount + 1)]
    largest = most if full else min(most, max(-(-total // amount), total * portions[0] // sum(portions)))
    least = 1 if total - largest >= amount - 1 else 0
    given, spare = [largest] + [least] * (amount - 1), total - largest - least * (amount - 1)
    while spare > 0:
        free = [i for i in range(1, amount) if given[i] < largest] or [i for i in range(1, amount) if given[i] < most]
        pool, left = sum([portions[i] for i in free]), spare
        for i in free:
            addition = min(most - given[i], max(1, left * portions[i] // pool), spare)
            given[i] = given[i] + addition
            spare = spare - addition
    return np.array(given)


def bell_draw(rng, dims, width, reach, split=(), held_as=jnp.bfloat16):
    values = width * jax.random.normal(rng, dims, jnp.float32)
    if split:
        values = values * block_levels(rng, dims, split, -0.22, 0.18)
    return jnp.clip(values, -reach, reach).astype(held_as)


def setup_inputs(seed: int = 0, part: int = 0) -> dict:
    keys = jax.random.split(jax.random.key(seed), 8)
    own_keys = jax.random.split(jax.random.fold_in(keys[7], part), 8)
    tokens = bell_draw(own_keys[0], (TOKENS, D), 1.0, 6.0, ((0, 16),))
    routes_keys = jax.random.split(jax.random.fold_in(own_keys[1], 1), TOKENS // TOK_DEV)
    routes_turns = jax.random.permutation(jax.random.fold_in(own_keys[1], 3), TOKENS // TOK_DEV)
    routes = jax.vmap(lambda own, number: deal_out(jax.random.fold_in(own_keys[1], 2), own, number, TOK_DEV, EXPERTS, TOPK, CAP, 2))(routes_keys, routes_turns).reshape((TOKENS, TOPK))
    route_weight = jnp.clip(jnp.exp(math.log(1.0) - 2.3025851 * jax.random.uniform(own_keys[2], (TOKENS, TOPK), jnp.float32) ** block_levels(own_keys[2], (TOKENS, TOPK), ((0, 16),), -0.2, 0.2)), 0.1, 1.0)
    norm_gain = jnp.clip(1.0 + 0.15 * jax.random.normal(keys[3], (D,), jnp.float32), 0.25, 1.75).astype(jnp.bfloat16)
    w_gate = bell_draw(keys[4], (N_EP, D, FFE_DEV), D ** -0.5, 0.09375, ((0, 16),))
    w_up = bell_draw(keys[5], (N_EP, D, FFE_DEV), D ** -0.5, 0.09375, ((0, 16),))
    w_down = bell_draw(keys[6], (N_EP, FFE_DEV, D), FFE ** -0.5, 0.1875, ((0, 16),))
    return {"tokens": tokens, "routes": routes, "route_weight": route_weight, "norm_gain": norm_gain, "w_gate": w_gate, "w_up": w_up, "w_down": w_down}


eps_norm = 1e-06

def normalize(tokens, norm_gain):
    values = tokens.astype(jnp.float32)
    inv_scale = lax.rsqrt(lax.optimization_barrier(jnp.mean(values * values, axis=-1, keepdims=True)) + eps_norm)
    return (values * inv_scale * norm_gain.astype(jnp.float32)).astype(jnp.bfloat16)

def expert_apply(expert_rows, gate_matrix, up_matrix, down_matrix):
    rows_wide = expert_rows.astype(jnp.float32)
    gate_act = jnp.dot(rows_wide, gate_matrix.astype(jnp.float32))
    up_act = jnp.dot(rows_wide, up_matrix.astype(jnp.float32))
    hidden = (jax.nn.silu(gate_act) * up_act).astype(jnp.bfloat16)
    return jnp.dot(hidden.astype(jnp.float32), down_matrix.astype(jnp.float32)).astype(jnp.bfloat16)

def reference(tokens, routes, route_weight, norm_gain, w_gate, w_up, w_down):
    normed = normalize(tokens, norm_gain)
    weights_wide = route_weight.astype(jnp.float32)

    def one_share(totals, holder):
        expert = (holder // SHARE).astype(jnp.int32)
        factor = lax.optimization_barrier(jnp.sum(jnp.where(routes == expert, weights_wide, jnp.zeros((), jnp.float32)), axis=1))
        result = expert_apply(normed, w_gate[holder], w_up[holder], w_down[holder])
        return (totals + result.astype(jnp.float32) * factor[:, None], None)
    totals, _ = lax.scan(one_share, jnp.zeros((TOKENS, D), jnp.float32), jnp.arange(N_EP, dtype=jnp.int32))
    return totals.astype(jnp.bfloat16)
```

```python
import functools

import jax
import jax.numpy as jnp
from jax import lax
from jax.experimental import pallas as pl
from jax.experimental.pallas import tpu as pltpu
from jax.sharding import PartitionSpec as P

FFE = 1024
MESH = pl.DeviceIdType.MESH
eps_norm = 1e-06
COL_CHUNKS = 4
DIAG_BY_Y = (True, True, True, False) + (True, True, True, False) * 2


def kernel(
    blocks, slot_rows,
    tok_ref, route_ref, rw_ref, gain_ref, wg_ref, wu_ref, wd_ref, out_ref,
    wgu, wdn, normed, packed, rows_in, hidden, part_own, part_send, part_recv, sum_send, sum_recv,
    local_sem, w_send, w_recv, c_send, c_recv, x_send, x_recv, p_send, p_recv, s_send, s_recv,
):
    toks, width = tok_ref.shape
    units = wg_ref.shape[1]
    me = lax.axis_index("ep")
    dp = lax.axis_index("dp")
    core = lax.rem(dp, 2)
    xb, yb, zb = lax.rem(me, 2), lax.rem(me // 2, 2), lax.rem(me // 4, 2)
    block = me // 8
    inner = lax.rem(me, 8)
    x_dev, y_dev, z_dev = me + 1 - 2 * xb, me + 2 - 4 * yb, me + 4 - 8 * zb
    dp_dev = dp + 1 - 2 * core
    m_own, m_y, m_z, m_d = zb * 2 + yb, zb * 2 + 1 - yb, (1 - zb) * 2 + yb, (1 - zb) * 2 + 1 - yb
    cols_n = width // COL_CHUNKS
    quarter = width // 4
    down_quarter = units // 4
    side = blocks * slot_rows

    def peer(r):
        return lax.rem(block + r, blocks)

    def cols(j):
        return pl.ds(j * cols_n, cols_n)

    def slot(index):
        return pl.ds(pl.multiple_of(index * slot_rows, 16), slot_rows)

    barrier = pltpu.get_barrier_semaphore()
    for other in (x_dev, y_dev, z_dev):
        pl.semaphore_signal(barrier, inc=1, device_id={"ep": other}, device_id_type=MESH)
    pl.semaphore_signal(barrier, inc=1, device_id={"dp": dp_dev}, device_id_type=MESH)
    for r in range(1, blocks):
        pl.semaphore_signal(
            barrier, inc=1, device_id={"ep": peer(r) * 8 + inner}, device_id_type=MESH
        )

    local = [
        pltpu.make_async_copy(wg_ref, wgu.at[m_own, :, pl.ds(0, units)], local_sem.at[0]),
        pltpu.make_async_copy(wu_ref, wgu.at[m_own, :, pl.ds(units, units)], local_sem.at[1]),
        pltpu.make_async_copy(
            wd_ref, wdn.at[pl.ds(pl.multiple_of(m_own * units, units), units), :], local_sem.at[2]
        ),
    ]
    for copy in local:
        copy.start()
    pl.semaphore_wait(barrier, 4 + blocks - 1)

    sent = []

    def remote(src, dst, ss, rs, where):
        return pltpu.make_async_remote_copy(
            src_ref=src, dst_ref=dst, send_sem=ss, recv_sem=rs, device_id=where,
            device_id_type=MESH,
        )

    def send(*args):
        copy = remote(*args)
        copy.start()
        sent.append(copy)

    def own_piece(k):
        if k < 4:
            ref = wu_ref if k % 2 else wg_ref
            first = core * (2 * quarter) + (k // 2) * quarter
            return ref.at[pl.ds(pl.multiple_of(first, 128), quarter), :]
        j, p = divmod(k - 4, 2)
        first = core * (2 * down_quarter) + p * down_quarter
        return wd_ref.at[pl.ds(pl.multiple_of(first, 16), down_quarter), cols(j)]

    def place(k, m, half):
        if k < 4:
            first = half * (2 * quarter) + (k // 2) * quarter
            return wgu.at[
                m, pl.ds(pl.multiple_of(first, 128), quarter), pl.ds((k % 2) * units, units)
            ]
        j, p = divmod(k - 4, 2)
        first = m * units + half * (2 * down_quarter) + p * down_quarter
        return wdn.at[pl.ds(pl.multiple_of(first, 16), down_quarter), cols(j)]

    def direct(k):
        for n, dev in ((0, y_dev), (1, z_dev)):
            send(own_piece(k), place(k, m_own, core), w_send.at[k, n], w_recv.at[k, n], {"ep": dev})

    def arrived(k, n, m, half):
        here = place(k, m, half)
        remote(here, here, w_send.at[k, n], w_recv.at[k, n], {"ep": y_dev}).wait_recv()

    def to_core(k, n, m):
        here = place(k, m, core)
        send(here, here, w_send.at[k, 3 + n], w_recv.at[k, 3 + n], {"dp": dp_dev})

    def relay(k):
        for n, m in ((0, m_y), (1, m_z)):
            arrived(k, n, m, core)
            to_core(k, n, m)
            if DIAG_BY_Y[k] == (n == 1):
                here = place(k, m, core)
                send(
                    here, here, w_send.at[k, 2], w_recv.at[k, 2],
                    {"ep": y_dev if DIAG_BY_Y[k] else z_dev},
                )

    def relay_diag(k):
        arrived(k, 2, m_d, core)
        to_core(k, 2, m_d)

    def from_core(k):
        for n, m in ((0, m_y), (1, m_z), (2, m_d)):
            here = place(k, m, 1 - core)
            remote(here, here, w_send.at[k, 3 + n], w_recv.at[k, 3 + n], {"dp": dp_dev}).wait_recv()

    for k in range(4):
        direct(k)

    total = jnp.zeros((toks, 128), jnp.float32)
    for i in range(width // 128):
        values = tok_ref[:, pl.ds(i * 128, 128)].astype(jnp.float32)
        total = total + values * values
    scale = lax.rsqrt(jnp.sum(total, axis=1, keepdims=True) / width + eps_norm)
    route = route_ref[...]
    later = lax.broadcasted_iota(jnp.int32, (toks, toks), 0)
    sooner = lax.broadcasted_iota(jnp.int32, (toks, toks), 1)
    before = (sooner < later).astype(jnp.float32).astype(jnp.bfloat16)
    rank = jnp.zeros((toks, 1), jnp.float32)
    for e in range(blocks):
        named = (route == e).astype(jnp.float32)
        wide = jnp.broadcast_to(named, (toks, 128)).astype(jnp.bfloat16)
        count = jnp.dot(before, wide, preferred_element_type=jnp.float32)
        rank = rank + named * count[:, :1]
    spot = route * slot_rows + rank.astype(jnp.int32)
    table = (lax.broadcasted_iota(jnp.int32, (toks, side), 1) == spot).astype(jnp.float32)
    table = table.astype(jnp.bfloat16)

    own_slot = slot(xb * blocks + block)
    for j in range(COL_CHUNKS):
        values = tok_ref[:, cols(j)].astype(jnp.float32)
        normed[...] = (values * scale * gain_ref[:, cols(j)].astype(jnp.float32)).astype(
            jnp.bfloat16
        )
        packed[:, cols(j)] = lax.dot_general(
            table, normed[...], (((0,), (0,)), ((), ())), preferred_element_type=jnp.float32
        ).astype(jnp.bfloat16)
        for r in range(1, blocks):
            send(
                packed.at[slot(peer(r)), cols(j)], rows_in.at[own_slot, cols(j)],
                c_send.at[j, r], c_recv.at[j, blocks - r], {"ep": peer(r) * 8 + inner},
            )
        send(
            packed.at[slot(block), cols(j)], rows_in.at[own_slot, cols(j)],
            x_send.at[j, 0], x_recv.at[j, 0], {"ep": x_dev},
        )
        rows_in[own_slot, cols(j)] = packed[slot(block), cols(j)]

    for j in range(COL_CHUNKS):
        relay(j)
        for r in range(1, blocks):
            here = rows_in.at[slot(xb * blocks + peer(r)), cols(j)]
            remote(here, here, c_send.at[j, r], c_recv.at[j, r], {"ep": x_dev}).wait_recv()
            send(here, here, x_send.at[j, r], x_recv.at[j, r], {"ep": x_dev})
        direct(4 + 2 * j)
        direct(5 + 2 * j)
    for k in range(4):
        relay_diag(k)
    relay(4)
    relay(5)

    for j in range(COL_CHUNKS):
        for r in range(blocks):
            here = rows_in.at[slot((1 - xb) * blocks + peer(r)), cols(j)]
            remote(here, here, x_send.at[j, r], x_recv.at[j, r], {"ep": x_dev}).wait_recv()
    for copy in local:
        copy.wait()
    for k in range(4):
        from_core(k)

    for m in range(4):
        acts = jnp.dot(rows_in[...], wgu[m], preferred_element_type=jnp.float32)
        gate, up = acts[:, :units], acts[:, units:]
        hidden[:, pl.ds(m * units, units)] = (gate / (1.0 + jnp.exp(-gate)) * up).astype(
            jnp.bfloat16
        )

    own_side = pl.ds(pl.multiple_of(xb * side, 16), side)
    other_side = pl.ds(pl.multiple_of((1 - xb) * side, 16), side)

    def give_back(j):
        here = part_recv.at[:, cols(j)]
        remote(here, here, p_send.at[j], p_recv.at[j], {"ep": x_dev}).wait_recv()
        sum_send[:, cols(j)] = (
            part_own[:, cols(j)] + part_recv[:, cols(j)].astype(jnp.float32)
        ).astype(jnp.bfloat16)
        for r in range(1, blocks):
            send(
                sum_send.at[slot(peer(r)), cols(j)], sum_recv.at[slot(block), cols(j)],
                s_send.at[j, r], s_recv.at[j, blocks - r], {"ep": peer(r) * 8 + inner},
            )
        sum_recv[slot(block), cols(j)] = sum_send[slot(block), cols(j)]

    for j in range(COL_CHUNKS):
        if j + 1 < COL_CHUNKS:
            relay(6 + 2 * j)
            relay(7 + 2 * j)
        for k in (4 + 2 * j, 5 + 2 * j):
            relay_diag(k)
        for k in (4 + 2 * j, 5 + 2 * j):
            from_core(k)
        part_send[:, cols(j)] = jnp.dot(
            hidden[other_side, :], wdn[:, cols(j)], preferred_element_type=jnp.float32
        ).astype(jnp.bfloat16)
        send(
            part_send.at[:, cols(j)], part_recv.at[:, cols(j)], p_send.at[j], p_recv.at[j],
            {"ep": x_dev},
        )
        part_own[:, cols(j)] = jnp.dot(
            hidden[own_side, :], wdn[:, cols(j)], preferred_element_type=jnp.float32
        )
        if j >= 1:
            give_back(j - 1)
    give_back(COL_CHUNKS - 1)

    factor = rw_ref[...]
    for j in range(COL_CHUNKS):
        for r in range(1, blocks):
            here = sum_recv.at[slot(peer(r)), cols(j)]
            remote(here, here, s_send.at[j, r], s_recv.at[j, r], {"ep": x_dev}).wait_recv()
        out_ref[:, cols(j)] = (
            jnp.dot(table, sum_recv[:, cols(j)], preferred_element_type=jnp.float32) * factor
        ).astype(jnp.bfloat16)
    for copy in sent:
        copy.wait_send()


def body(tokens, routes, route_weight, norm_gain, w_gate, w_up, w_down):
    toks, width = tokens.shape
    units = w_gate.shape[2]
    blocks = lax.axis_size("ep") // (FFE // units)
    cap_rows = max(2, toks * 9 // (8 * blocks))
    slot_rows = -(-cap_rows // 16) * 16
    side = blocks * slot_rows
    vmem = pl.BlockSpec(memory_space=pltpu.VMEM)
    hbm = pl.BlockSpec(memory_space=pl.ANY)
    dma = pltpu.SemaphoreType.DMA
    pieces = 4 + 2 * COL_CHUNKS
    return pl.pallas_call(
        functools.partial(kernel, blocks, slot_rows),
        out_shape=jax.ShapeDtypeStruct((toks, width), jnp.bfloat16),
        in_specs=[vmem] * 4 + [hbm] * 3,
        out_specs=vmem,
        scratch_shapes=[
            pltpu.VMEM((4, width, 2 * units), jnp.bfloat16),
            pltpu.VMEM((4 * units, width), jnp.bfloat16),
            pltpu.VMEM((toks, width // COL_CHUNKS), jnp.bfloat16),
            pltpu.VMEM((side, width), jnp.bfloat16),
            pltpu.VMEM((2 * side, width), jnp.bfloat16),
            pltpu.VMEM((2 * side, 4 * units), jnp.bfloat16),
            pltpu.VMEM((side, width), jnp.float32),
            pltpu.VMEM((side, width), jnp.bfloat16),
            pltpu.VMEM((side, width), jnp.bfloat16),
            pltpu.VMEM((side, width), jnp.bfloat16),
            pltpu.VMEM((side, width), jnp.bfloat16),
            dma((3,)),
            dma((pieces, 6)),
            dma((pieces, 6)),
            dma((COL_CHUNKS, blocks)),
            dma((COL_CHUNKS, blocks)),
            dma((COL_CHUNKS, blocks)),
            dma((COL_CHUNKS, blocks)),
            dma((COL_CHUNKS,)),
            dma((COL_CHUNKS,)),
            dma((COL_CHUNKS, blocks)),
            dma((COL_CHUNKS, blocks)),
        ],
        compiler_params=pltpu.CompilerParams(
            collective_id=0, has_side_effects=True, vmem_limit_bytes=48 * 1024 * 1024
        ),
        cost_estimate=pl.CostEstimate(
            flops=2 * 2 * side * width * 12 * units, bytes_accessed=8 << 20, transcendentals=0
        ),
    )(
        tokens, routes, route_weight, norm_gain.reshape(1, width), w_gate[0], w_up[0], w_down[0]
    )


def solution(mesh):
    in_specs = (
        P(("dp", "ep"), None),
        P(("dp", "ep"), None),
        P(("dp", "ep"), None),
        P(),
        P("ep", None, None),
        P("ep", None, None),
        P("ep", None, None),
    )
    out_specs = P(("dp", "ep"), None)
    return jax.shard_map(body, mesh=mesh, in_specs=in_specs, out_specs=out_specs, check_vma=False)
```

```python
import functools

import jax
import jax.numpy as jnp
from jax import lax
from jax.experimental import pallas as pl
from jax.experimental.pallas import tpu as pltpu
from jax.sharding import PartitionSpec as P

FFE = 1024
MESH = pl.DeviceIdType.MESH
eps_norm = 1e-06
CHUNKS = (2, 4, 4, 2, 2)
DIAG_BY_Y = (True, True, True, False) + (True, True, True, False, True) * 2


def kernel(
    blocks, half_rows,
    tok_ref, route_ref, rw_ref, gain_ref, wg_ref, wu_ref, wd_ref, out_ref,
    tok_in, wgu, wdn, packed, rows_in, hidden, part_own, part_send, part_recv, sum_send, sum_recv,
    local_sem, w_send, w_recv, c_send, c_recv, x_send, x_recv, p_send, p_recv, s_send, s_recv,
):
    toks, width = tok_ref.shape
    half = width // 2
    slot_rows = 2 * half_rows
    units = wg_ref.shape[1]
    me = lax.axis_index("ep")
    dp = lax.axis_index("dp")
    core = lax.rem(dp, 2)
    xb, yb, zb = lax.rem(me, 2), lax.rem(me // 2, 2), lax.rem(me // 4, 2)
    block = me // 8
    inner = lax.rem(me, 8)
    x_dev, y_dev, z_dev = me + 1 - 2 * xb, me + 2 - 4 * yb, me + 4 - 8 * zb
    dp_dev = dp + 1 - 2 * core
    m_own, m_y, m_z, m_d = zb * 2 + yb, zb * 2 + 1 - yb, (1 - zb) * 2 + yb, (1 - zb) * 2 + 1 - yb
    last = len(CHUNKS) - 1
    quarter = width // 4
    down_rows = units // 2
    side = blocks * slot_rows

    def peer(r):
        return lax.rem(block + r, blocks)

    def cols(j, h=0):
        return pl.ds(h * half + sum(CHUNKS[:j]) * 128, CHUNKS[j] * 128)

    def slot(index):
        return pl.ds(pl.multiple_of(index * slot_rows, 16), slot_rows)

    barrier = pltpu.get_barrier_semaphore()
    for other in (x_dev, y_dev, z_dev):
        pl.semaphore_signal(barrier, inc=1, device_id={"ep": other}, device_id_type=MESH)
    pl.semaphore_signal(barrier, inc=1, device_id={"dp": dp_dev}, device_id_type=MESH)
    for r in range(1, blocks):
        pl.semaphore_signal(
            barrier, inc=1, device_id={"ep": peer(r) * 8 + inner}, device_id_type=MESH
        )

    local = [
        pltpu.make_async_copy(wg_ref, wgu.at[m_own, :, pl.ds(0, units)], local_sem.at[0]),
        pltpu.make_async_copy(wu_ref, wgu.at[m_own, :, pl.ds(units, units)], local_sem.at[1]),
        pltpu.make_async_copy(
            wd_ref, wdn.at[pl.ds(pl.multiple_of(m_own * units, units), units), :], local_sem.at[2]
        ),
    ]
    tok_copy = pltpu.make_async_copy(tok_ref, tok_in, local_sem.at[3])
    tok_copy.start()
    for copy in local:
        copy.start()
    pl.semaphore_wait(barrier, 4 + blocks - 1)

    sent = []

    def remote(src, dst, ss, rs, where):
        return pltpu.make_async_remote_copy(
            src_ref=src, dst_ref=dst, send_sem=ss, recv_sem=rs, device_id=where,
            device_id_type=MESH,
        )

    def send(*args):
        copy = remote(*args)
        copy.start()
        sent.append(copy)

    def own_piece(k):
        if k < 4:
            ref = wu_ref if k % 2 else wg_ref
            first = core * (2 * quarter) + (k // 2) * quarter
            return ref.at[pl.ds(pl.multiple_of(first, 128), quarter), :]
        j, p = divmod(k - 4, 2)
        first = core * down_rows
        return wd_ref.at[pl.ds(pl.multiple_of(first, 16), down_rows), cols(j, p)]

    def place(k, m, part):
        if k < 4:
            first = part * (2 * quarter) + (k // 2) * quarter
            return wgu.at[
                m, pl.ds(pl.multiple_of(first, 128), quarter), pl.ds((k % 2) * units, units)
            ]
        j, p = divmod(k - 4, 2)
        first = m * units + part * down_rows
        return wdn.at[pl.ds(pl.multiple_of(first, 16), down_rows), cols(j, p)]

    def direct(k, n):
        send(
            own_piece(k), place(k, m_own, core), w_send.at[k, n], w_recv.at[k, n],
            {"ep": (y_dev, z_dev)[n]},
        )

    def arrived(k, n, m, part):
        here = place(k, m, part)
        remote(here, here, w_send.at[k, n], w_recv.at[k, n], {"ep": y_dev}).wait_recv()

    def to_core(k, n, m):
        here = place(k, m, core)
        send(here, here, w_send.at[k, 3 + n], w_recv.at[k, 3 + n], {"dp": dp_dev})

    def relay(k, n):
        m = (m_y, m_z)[n]
        arrived(k, n, m, core)
        to_core(k, n, m)
        if DIAG_BY_Y[k] == (n == 1):
            here = place(k, m, core)
            send(
                here, here, w_send.at[k, 2], w_recv.at[k, 2],
                {"ep": y_dev if DIAG_BY_Y[k] else z_dev},
            )

    def relay_diag(k):
        arrived(k, 2, m_d, core)
        to_core(k, 2, m_d)

    def from_core(k, n, m):
        here = place(k, m, 1 - core)
        remote(here, here, w_send.at[k, 3 + n], w_recv.at[k, 3 + n], {"dp": dp_dev}).wait_recv()

    def down(step, j, *rest):
        step(4 + 2 * j, *rest)
        step(5 + 2 * j, *rest)

    for k in (0, 1, 2, 4, 5, 3):
        direct(k, 1)
        direct(k, 0)
    tok_copy.wait()

    def as_column(line):
        down_index = lax.broadcasted_iota(jnp.int32, (toks, toks), 0)
        across = lax.broadcasted_iota(jnp.int32, (toks, toks), 1)
        square = jnp.where(down_index == across, jnp.broadcast_to(line, (toks, toks)), 0.0)
        return jnp.sum(square, axis=1, keepdims=True)

    total = jnp.zeros((toks, 128), jnp.float32)
    for i in range(width // 128):
        values = tok_in[:, pl.ds(i * 128, 128)].astype(jnp.float32)
        total = total + values * values
    scale = lax.rsqrt(jnp.sum(total, axis=1, keepdims=True) / width + eps_norm)
    route = as_column(route_ref[...].astype(jnp.float32)).astype(jnp.int32)
    later = lax.broadcasted_iota(jnp.int32, (toks, toks), 0)
    sooner = lax.broadcasted_iota(jnp.int32, (toks, toks), 1)
    before = (sooner < later).astype(jnp.float32).astype(jnp.bfloat16)
    rank = jnp.zeros((toks, 1), jnp.float32)
    for e in range(blocks):
        named = (route == e).astype(jnp.float32)
        wide = jnp.broadcast_to(named, (toks, 128)).astype(jnp.bfloat16)
        count = jnp.dot(before, wide, preferred_element_type=jnp.float32)
        rank = rank + named * count[:, :1]
    tables = []
    for h in range(2):
        spot = route * slot_rows + h * half_rows + rank.astype(jnp.int32)
        one = (lax.broadcasted_iota(jnp.int32, (toks, side), 1) == spot).astype(jnp.float32)
        tables.append(one.astype(jnp.bfloat16))

    own_slot = slot(xb * blocks + block)
    for j in range(last + 1):
        total = jnp.zeros((side, CHUNKS[j] * 128), jnp.float32)
        for h in range(2):
            values = tok_in[:, cols(j, h)].astype(jnp.float32)
            normed = (values * scale * gain_ref[:, cols(j, h)].astype(jnp.float32)).astype(
                jnp.bfloat16
            )
            total = total + lax.dot_general(
                tables[h], normed, (((0,), (0,)), ((), ())), preferred_element_type=jnp.float32
            )
        packed[:, cols(j)] = total.astype(jnp.bfloat16)
        for r in range(1, blocks):
            send(
                packed.at[slot(peer(r)), cols(j)], rows_in.at[own_slot, cols(j)],
                c_send.at[j, r], c_recv.at[j, blocks - r], {"ep": peer(r) * 8 + inner},
            )
        send(
            packed.at[slot(block), cols(j)], rows_in.at[own_slot, cols(j)],
            x_send.at[j, 0], x_recv.at[j, 0], {"ep": x_dev},
        )
        rows_in[own_slot, cols(j)] = packed[slot(block), cols(j)]

    def relay_rows(j):
        for r in range(1, blocks):
            here = rows_in.at[slot(xb * blocks + peer(r)), cols(j)]
            remote(here, here, c_send.at[j, r], c_recv.at[j, r], {"ep": x_dev}).wait_recv()
            send(here, here, x_send.at[j, r], x_recv.at[j, r], {"ep": x_dev})

    def acts(m):
        low = jnp.dot(rows_in[...], wgu[m, :half, :], preferred_element_type=jnp.float32)
        high = jnp.dot(rows_in[...], wgu[m, half:, :], preferred_element_type=jnp.float32)
        parts = []
        for i in range(2 * blocks):
            first = i * slot_rows
            both = low[first:first + half_rows] + high[first + half_rows:first + slot_rows]
            gate, up = both[:, :units], both[:, units:]
            parts.append(gate / (1.0 + jnp.exp(-gate)) * up)
        hidden[m] = jnp.concatenate(parts, axis=0).astype(jnp.bfloat16)

    relay(0, 0)
    relay(0, 1)
    relay_rows(0)
    relay(1, 0)
    relay(2, 0)
    relay(1, 1)
    relay_rows(1)
    relay_diag(0)
    down(relay, 0, 0)
    relay(3, 0)
    relay(2, 1)
    relay_rows(2)
    relay_diag(1)
    down(relay, 0, 1)
    for j in range(3, last + 1):
        relay_rows(j)
    relay(3, 1)
    down(direct, 1, 0)
    down(direct, 1, 1)
    for j in range(last + 1):
        for r in range(blocks):
            here = rows_in.at[slot((1 - xb) * blocks + peer(r)), cols(j)]
            remote(here, here, x_send.at[j, r], x_recv.at[j, r], {"ep": x_dev}).wait_recv()
    for copy in local:
        copy.wait()
    acts(m_own)
    relay_diag(2)
    for k in range(4):
        from_core(k, 0, m_y)
    acts(m_y)
    down(relay_diag, 0)
    relay_diag(3)
    for j in range(2, last + 1):
        down(direct, j, 0)
        down(direct, j, 1)
    for k in range(4):
        from_core(k, 1, m_z)
    acts(m_z)
    down(relay, 1, 0)
    down(relay, 1, 1)
    for k in range(4):
        from_core(k, 2, m_d)
    acts(m_d)

    own_side = pl.ds(pl.multiple_of(xb * blocks * half_rows, 16), blocks * half_rows)
    other_side = pl.ds(pl.multiple_of((1 - xb) * blocks * half_rows, 16), blocks * half_rows)

    def partial(rows, j):
        ends = []
        for h in range(2):
            total = jnp.zeros((blocks * half_rows, CHUNKS[j] * 128), jnp.float32)
            for m in range(4):
                total = total + jnp.dot(
                    hidden[m, rows, :], wdn[pl.ds(m * units, units), cols(j, h)],
                    preferred_element_type=jnp.float32,
                )
            ends.append(total)
        pieces = []
        for e in range(blocks):
            for h in range(2):
                pieces.append(ends[h][e * half_rows:(e + 1) * half_rows])
        return jnp.concatenate(pieces, axis=0)

    def give_back(j):
        here = part_recv.at[:, cols(j)]
        remote(here, here, p_send.at[j], p_recv.at[j], {"ep": x_dev}).wait_recv()
        sum_send[:, cols(j)] = (
            part_own[:, cols(j)] + part_recv[:, cols(j)].astype(jnp.float32)
        ).astype(jnp.bfloat16)
        for r in range(1, blocks):
            send(
                sum_send.at[slot(peer(r)), cols(j)], sum_recv.at[slot(block), cols(j)],
                s_send.at[j, r], s_recv.at[j, blocks - r], {"ep": peer(r) * 8 + inner},
            )
        sum_recv[slot(block), cols(j)] = sum_send[slot(block), cols(j)]

    for j in range(last + 1):
        for n, m in ((0, m_y), (1, m_z), (2, m_d)):
            down(lambda k: from_core(k, n, m), j)
        part_send[:, cols(j)] = partial(other_side, j).astype(jnp.bfloat16)
        send(
            part_send.at[:, cols(j)], part_recv.at[:, cols(j)], p_send.at[j], p_recv.at[j],
            {"ep": x_dev},
        )
        part_own[:, cols(j)] = partial(own_side, j)
        if j >= 1:
            give_back(j - 1)
        if j < last:
            down(relay_diag, j + 1)
        if j + 1 < last:
            down(relay, j + 2, 0)
            down(relay, j + 2, 1)
    give_back(last)

    factor = as_column(rw_ref[...])
    for j in range(last + 1):
        for r in range(1, blocks):
            here = sum_recv.at[slot(peer(r)), cols(j)]
            remote(here, here, s_send.at[j, r], s_recv.at[j, r], {"ep": x_dev}).wait_recv()
        for h in range(2):
            out_ref[:, cols(j, h)] = (
                jnp.dot(tables[h], sum_recv[:, cols(j)], preferred_element_type=jnp.float32)
                * factor
            ).astype(jnp.bfloat16)
    for copy in sent:
        copy.wait_send()


def body(tokens, routes, route_weight, norm_gain, w_gate, w_up, w_down):
    toks, width = tokens.shape
    units = w_gate.shape[2]
    blocks = lax.axis_size("ep") // (FFE // units)
    cap_rows = max(2, toks * 9 // (8 * blocks))
    half_rows = -(-cap_rows // 8) * 8
    side = blocks * 2 * half_rows
    half = width // 2
    chunks = len(CHUNKS)
    vmem = pl.BlockSpec(memory_space=pltpu.VMEM)
    hbm = pl.BlockSpec(memory_space=pl.ANY)
    dma = pltpu.SemaphoreType.DMA
    pieces = 4 + 2 * chunks
    return pl.pallas_call(
        functools.partial(kernel, blocks, half_rows),
        out_shape=jax.ShapeDtypeStruct((toks, width), jnp.bfloat16),
        in_specs=[hbm] + [vmem] * 3 + [hbm] * 3,
        out_specs=vmem,
        scratch_shapes=[
            pltpu.VMEM((toks, width), jnp.bfloat16),
            pltpu.VMEM((4, width, 2 * units), jnp.bfloat16),
            pltpu.VMEM((4 * units, width), jnp.bfloat16),
            pltpu.VMEM((side, half), jnp.bfloat16),
            pltpu.VMEM((2 * side, half), jnp.bfloat16),
            pltpu.VMEM((4, side, units), jnp.bfloat16),
            pltpu.VMEM((side, half), jnp.float32),
            pltpu.VMEM((side, half), jnp.bfloat16),
            pltpu.VMEM((side, half), jnp.bfloat16),
            pltpu.VMEM((side, half), jnp.bfloat16),
            pltpu.VMEM((side, half), jnp.bfloat16),
            dma((4,)),
            dma((pieces, 6)),
            dma((pieces, 6)),
            dma((chunks, blocks)),
            dma((chunks, blocks)),
            dma((chunks, blocks)),
            dma((chunks, blocks)),
            dma((chunks,)),
            dma((chunks,)),
            dma((chunks, blocks)),
            dma((chunks, blocks)),
        ],
        compiler_params=pltpu.CompilerParams(
            collective_id=0, has_side_effects=True, vmem_limit_bytes=60 * 1024 * 1024
        ),
        cost_estimate=pl.CostEstimate(
            flops=2 * 2 * side * width * 12 * units, bytes_accessed=8 << 20, transcendentals=0
        ),
    )(
        tokens, routes.reshape(1, toks), route_weight.reshape(1, toks), norm_gain.reshape(1, width), w_gate[0], w_up[0], w_down[0]
    )


def solution(mesh):
    in_specs = (
        P(("dp", "ep"), None),
        P(("dp", "ep"), None),
        P(("dp", "ep"), None),
        P(),
        P("ep", None, None),
        P("ep", None, None),
        P("ep", None, None),
    )
    out_specs = P(("dp", "ep"), None)
    return jax.shard_map(body, mesh=mesh, in_specs=in_specs, out_specs=out_specs, check_vma=False)
```
